128 devices in a mesh: row: 16 (over z, y_hi, core), col: 8 (over x, y_lo).
Axes of the slice: x: 4, y: 4 (y_hi: 2, y_lo: 2; y = y_hi * 2 + y_lo), z: 4, core: 2. Of those that a mesh axis runs over, the one named last changes fastest.
Arguments:
- features: bfloat16 [65536, 256], P(('row', 'col')), may hold values from -6 to 6
- tile_values: bfloat16 [16, 8, 512, 128, 128], P('row', 'col'), may hold values from 0 to 1, as said below
- tile_index: int32 [16, 8, 512], P('row', 'col'), may hold values from 0 to 2047, as said below
- tile_count: int32 [16, 8], P('row', 'col'), may hold values from 64 to 512
- weight: bfloat16 [256, 256], replicated, may hold values from -0.375 to 0.375
- out_bias: float32 [256], replicated, may hold values from -3 to 3
Outputs:
- layer_out: bfloat16 [65536, 256], P(('row', 'col'))
The draws below stay inside these ranges and needn't reach their ends.
Inputs may be any that keep to these rules, and one draw needn't show every extreme that they name: `tile_index`: in each grid block the first tile_count entries name distinct tiles. `tile_values`: edge weights are bfloat16 values in [0, 1).
All inputs are finite; a program needn't handle non-finite values.
Results may differ from the reference program's by a relative error of at most 0.0047.
Values may be sent and summed in bfloat16 or wider, within the bound.
A program may use at most 128 MiB of HBM per device.

```python
import jax
import jax.numpy as jnp
from jax import lax

F = 256
TILE = 128
VP = 512
N = 65536
ROW_TILES = 32
COL_TILES = 64
MAXT = 512
N_ROW = 16
N_COL = 8


def draw_tile_values(key, part):
    key_q = jax.random.fold_in(jax.random.fold_in(key, 11), 0)
    shape = (N_ROW, N_COL, MAXT, TILE, TILE)
    levels = jax.random.randint(key_q, shape, 0, 256).astype(jnp.float32) / 256.0
    return levels.astype(jnp.bfloat16)


def draw_tile_index(key, part):
    keys = jax.random.split(jax.random.fold_in(key, 23), N_ROW * N_COL)
    grid_size = ROW_TILES * COL_TILES
    picked = jax.vmap(lambda one_key: jax.random.permutation(one_key, grid_size)[:MAXT])(keys)
    return picked.reshape(N_ROW, N_COL, MAXT).astype(jnp.int32)


def draw_tile_count(key, part):
    key_a, key_b, key_c, key_d = jax.random.split(jax.random.fold_in(key, 37), 4)
    light = jax.random.randint(key_a, (N_ROW, N_COL), MAXT // 8, MAXT // 4 + 1)
    heavy = jax.random.randint(key_b, (N_ROW, N_COL), MAXT // 2, MAXT + 1)
    hub_rows = jax.random.permutation(key_c, N_ROW)[:2]
    row_ids = jnp.arange(N_ROW, dtype=jnp.int32)
    col_ids = jnp.arange(N_COL, dtype=jnp.int32)
    is_hub = jnp.any(row_ids[:, None] == hub_rows[None, :], axis=1)
    counts = jnp.where(is_hub[:, None], heavy, light)
    top_col = jax.random.randint(key_d, (), 0, N_COL)
    top_cell = (row_ids[:, None] == hub_rows[0]) & (col_ids[None, :] == top_col)
    return jnp.where(top_cell, MAXT, counts).astype(jnp.int32)


def block_levels(own_key, dims, cuts, least, high):
    factor_of = 1.0
    for position, blocks in cuts:
        steps = jax.random.uniform(jax.random.fold_in(jax.random.fold_in(own_key, 6), position), (blocks,), jnp.float32, least / len(cuts), high / len(cuts))
        factor_of = factor_of * jnp.repeat(jnp.exp(steps), dims[position] // blocks).reshape((-1,) + (1,) * (len(dims) - 1 - position))
    return factor_of


def bell_draw(own_key, extent, scale, most, pieces=(), held_as=jnp.bfloat16):
    gain = block_levels(own_key, extent, pieces, -0.22, 0.18) if pieces else 1.0
    values = jax.random.normal(own_key, extent, jnp.float32) * scale * gain
    return jnp.minimum(jnp.maximum(values, -most), most).astype(held_as)


def setup_inputs(seed: int = 0) -> dict:
    seeds = jax.random.split(jax.random.key(seed), 7)
    return {
        "features": bell_draw(seeds[0], (N, F), 1.0, 6.0, ((0, 128),)),
        "tile_values": draw_tile_values(jax.random.fold_in(seeds[6], 71), 0),
        "tile_index": draw_tile_index(jax.random.fold_in(seeds[6], 71), 0),
        "tile_count": draw_tile_count(jax.random.fold_in(seeds[6], 71), 0),
        "weight": bell_draw(seeds[4], (F, F), F ** -0.5, 0.375),
        "out_bias": bell_draw(seeds[5], (F,), 0.5, 3.0, (), jnp.float32),
    }


def reference(features, tile_values, tile_index, tile_count, weight, out_bias):
    col_tiles = N_ROW * VP // TILE
    row_tiles = N_COL * VP // TILE
    group_size = min(32, MAXT)
    blocks = features.reshape(N_ROW, N_COL, VP, F)

    def one_device(dev_id, carry):
        acc_total, degree = carry
        row_id = dev_id // N_COL
        col_id = dev_id % N_COL
        column = lax.dynamic_index_in_dim(blocks, col_id, 1, keepdims=False).reshape(col_tiles, TILE, F)
        slot_values = lax.dynamic_index_in_dim(lax.dynamic_index_in_dim(tile_values, row_id, 0, False), col_id, 0, False)
        positions = lax.dynamic_index_in_dim(lax.dynamic_index_in_dim(tile_index, row_id, 0, False), col_id, 0, False)
        live_count = tile_count[row_id, col_id]
        turn_count = (live_count + group_size - 1) // group_size

        def one_turn(turn_id, inner_carry):
            part_total, part_degree = inner_carry
            turn_begin = (turn_id * group_size).astype(jnp.int32)
            first_slot = jnp.minimum(turn_begin, MAXT - group_size).astype(jnp.int32)
            tile_block = lax.dynamic_slice_in_dim(slot_values, first_slot, group_size, 0).astype(jnp.float32)
            slot_pos = lax.dynamic_slice_in_dim(positions, first_slot, group_size, 0)
            slot_ids = first_slot + jnp.arange(group_size, dtype=jnp.int32)
            live_mask = ((slot_ids >= turn_begin) & (slot_ids < live_count)).astype(jnp.float32)
            tile_rows = slot_pos // col_tiles
            tile_cols = slot_pos % col_tiles
            sources = column[tile_cols].astype(jnp.float32)
            products = jnp.einsum('gij,gjf->gif', tile_block, sources) * live_mask[:, None, None]
            row_sums = lax.optimization_barrier(jnp.sum(tile_block, axis=2)) * live_mask[:, None]
            return (part_total.at[tile_rows].add(products), part_degree.at[tile_rows].add(row_sums))
        zeros_init = (jnp.zeros((row_tiles, TILE, F), jnp.float32), jnp.zeros((row_tiles, TILE), jnp.float32))
        part_total, part_degree = lax.fori_loop(0, turn_count, one_turn, zeros_init)
        acc_total = acc_total.at[row_id].add(part_total)
        degree = degree.at[row_id].add(part_degree)
        return (acc_total, degree)
    start_carry = (jnp.zeros((N_ROW, row_tiles, TILE, F), jnp.float32), jnp.zeros((N_ROW, row_tiles, TILE), jnp.float32))
    acc_total, degree = lax.fori_loop(0, N_ROW * N_COL, one_device, start_carry)
    aggregate = acc_total.reshape(N, F)
    degree = degree.reshape(N)
    hidden = (aggregate * lax.rsqrt(1.0 + degree)[:, None] + features.astype(jnp.float32)).astype(jnp.bfloat16)
    mixed = jnp.dot(hidden, weight, preferred_element_type=jnp.float32) + out_bias.astype(jnp.float32)
    return jnp.maximum(mixed, 0.0).astype(jnp.bfloat16)
```

```python
import jax
import jax.numpy as jnp
from jax import lax
from jax.experimental import pallas as pl
from jax.experimental.pallas import tpu as pltpu
from jax.sharding import PartitionSpec as P

TILE = 128
F = 256
VP = 512
HALF = VP // 2
SLOTS = 512
PIECES = 16
OWNERS = 8
CHUNKS = 8
PER_CHUNK = SLOTS // CHUNKS
MESH = pl.DeviceIdType.MESH

N_GATHER = 19
N_REDUCE = 7


def kernel(
    count_ref, index_ref, features_ref, values_ref, weight_ref, bias_ref,
    out_ref,
    tiles, gathered, acc, sent, received, degree, degree_in, scale, inverse_v, inverse,
    load_sem, own_sem, inverse_sem, gs_sem, gr_sem, rs_sem, rr_sem, ds_sem, dr_sem,
):
    row = lax.axis_index("row")
    col = lax.axis_index("col")
    z, yh, core = row // 4, (row // 2) % 2, row % 2
    x, yl = col // 2, col % 2

    def in_row_group(dx, dy):
        xo = (x + dx) % 4
        yo = (yl + dy) % 2
        return {"row": row, "col": xo * 2 + yo}

    def in_col_group(dz, dy, dk):
        return {"row": ((z + dz) % 4) * 4 + ((yh + dy) % 2) * 2 + (core + dk) % 2, "col": col}

    def piece(dz, dy, dk=0):
        return ((z + dz) % 4) * 4 + ((yh + dy) % 2) * 2 + (core + dk) % 2

    loads = []
    for i in range(CHUNKS):
        part = pl.ds(i * PER_CHUNK, PER_CHUNK)
        loads.append(pltpu.make_async_copy(values_ref.at[part], tiles.at[part], load_sem.at[i]))
        loads[-1].start()
    own_copy = pltpu.make_async_copy(features_ref, gathered.at[row], own_sem)
    own_copy.start()

    others = [(dx, dy) for dx in range(4) for dy in range(2) if (dx, dy) != (0, 0)]
    barrier = pltpu.get_barrier_semaphore()
    near = [in_col_group(0, 0, 1), in_col_group(1, 0, 0), in_col_group(3, 0, 0), in_col_group(0, 1, 0)]
    far = [in_row_group(dx, dy) for dx, dy in others]
    for device in near + far:
        pl.semaphore_signal(barrier, inc=1, device_id=device, device_id_type=MESH)
    pl.semaphore_wait(barrier, len(near) + len(far))

    sends = []

    def remote(src, dst, send_sem, recv_sem, device):
        copy = pltpu.make_async_remote_copy(
            src_ref=src, dst_ref=dst, send_sem=send_sem, recv_sem=recv_sem,
            device_id=device, device_id_type=MESH,
        )
        copy.start()
        sends.append(copy)
        return copy

    def part_of(which, half):
        if half is None:
            return gathered.at[which]
        return gathered.at[which, pl.ds(half * HALF, HALF)]

    gather_count = [0]

    def gather_send(which, half, role, device, src=None):
        place = part_of(which, half)
        n = gather_count[0]
        gather_count[0] += 1
        remote(place if src is None else src, place, gs_sem.at[n], gr_sem.at[role], device)

    def gather_wait(which, half, role):
        place = part_of(which, half)
        pltpu.make_async_remote_copy(
            src_ref=place, dst_ref=place, send_sem=gs_sem.at[0], recv_sem=gr_sem.at[role],
            device_id=near[0], device_id_type=MESH,
        ).wait_recv()

    sibling, z_up, z_down, y_far = near

    gather_send(row, None, 1, z_up, features_ref)
    gather_send(row, None, 2, z_down, features_ref)
    gather_send(row, None, 3, y_far, features_ref)
    gather_send(row, None, 0, sibling, features_ref)

    live = count_ref[0]
    tiles[SLOTS] = jnp.zeros((TILE, TILE), jnp.bfloat16)
    place_id = (
        lax.broadcasted_iota(jnp.int32, (16, TILE), 0) * TILE
        + lax.broadcasted_iota(jnp.int32, (16, TILE), 1)
    )

    def mark(step, found):
        for u in range(16):
            slot = step * 16 + u
            position = jnp.where(slot < live, index_ref[slot], -1)
            found = jnp.where(place_id == position, slot, found)
        return found

    inverse_v[...] = lax.fori_loop(0, SLOTS // 16, mark, jnp.full((16, TILE), SLOTS, jnp.int32))
    inverse_copy = pltpu.make_async_copy(inverse_v, inverse, inverse_sem)
    inverse_copy.start()

    row_id = lax.broadcasted_iota(jnp.int32, (OWNERS * 8, TILE), 0)
    degree[...] = jnp.zeros_like(degree)
    for i in range(CHUNKS):
        loads[i].wait()
        marks, parts = [], []
        for u in range(PER_CHUNK):
            slot = i * PER_CHUNK + u
            tile_row = index_ref[slot] // 64
            at = jnp.where(slot < live, (tile_row // 4) * 8 + tile_row % 4, -1)
            marks.append((row_id == at).astype(jnp.float32).astype(jnp.bfloat16))
            parts.append(tiles[slot])
        sums = lax.dot_general(
            jnp.concatenate(marks, axis=1), jnp.concatenate(parts, axis=1),
            (((1,), (1,)), ((), ())), preferred_element_type=jnp.float32,
        )
        degree[...] += sums.reshape(degree.shape)

    for n, (dx, dy) in enumerate(others):
        target = ((x + dx) % 4) * 2 + (yl + dy) % 2
        remote(degree.at[target], degree_in.at[n], ds_sem.at[n], dr_sem.at[n], in_row_group(dx, dy))
    inverse_copy.wait()
    own_copy.wait()

    def block_of_a(first_row, rows, pieces):
        half_row = first_row // 2
        lines = []
        for a in range(rows):
            line = []
            for p in pieces:
                for b in range(4):
                    lane = (a % 2) * 64 + p * 4 + b
                    line.append(tiles[inverse[half_row + a // 2, lane]])
            lines.append(jnp.concatenate(line, axis=1))
        return jnp.concatenate(lines, axis=0)

    def product(first_row, rows, pieces):
        sources = jnp.concatenate([gathered[p] for p in pieces], axis=0)
        return jnp.dot(
            block_of_a(first_row, rows, pieces), sources, preferred_element_type=jnp.float32
        )

    def accumulate(pieces, first):
        def step(i, _):
            span = pl.ds(pl.multiple_of(i * 8 * TILE, 8 * TILE), 8 * TILE)
            value = product(i * 8, 8, pieces)
            acc[span, :] = value if first else acc[span, :] + value
            return 0

        lax.fori_loop(0, 4, step, 0)

    gather_wait(piece(0, 0, 1), None, 0)
    accumulate([piece(0, 0), piece(0, 0, 1)], True)

    gather_wait(piece(3, 0), None, 1)
    gather_send(piece(3, 0), 0, 4, z_up)
    gather_wait(piece(1, 0), None, 2)
    gather_send(piece(1, 0), 1, 5, z_down)
    gather_send(piece(3, 0), None, 10, sibling)
    gather_send(piece(1, 0), None, 11, sibling)
    gather_wait(piece(0, 1), None, 3)
    gather_send(piece(0, 1), None, 6, z_up)
    gather_send(piece(0, 1), None, 7, z_down)
    gather_send(piece(0, 1), None, 12, sibling)

    gather_wait(piece(3, 0, 1), None, 10)
    accumulate([piece(3, 0), piece(3, 0, 1)], False)

    gather_wait(piece(2, 0), 0, 4)
    gather_send(piece(2, 0), 0, 8, y_far)
    gather_wait(piece(2, 0), 1, 5)
    gather_send(piece(2, 0), 1, 9, y_far)
    gather_send(piece(2, 0), 0, 13, sibling)
    gather_send(piece(2, 0), 1, 14, sibling)

    gather_wait(piece(1, 0, 1), None, 11)
    accumulate([piece(1, 0), piece(1, 0, 1)], False)
    gather_wait(piece(0, 1, 1), None, 12)
    accumulate([piece(0, 1), piece(0, 1, 1)], False)

    gather_wait(piece(3, 1), None, 6)
    gather_send(piece(3, 1), None, 15, sibling)
    gather_wait(piece(1, 1), None, 7)
    gather_send(piece(1, 1), None, 16, sibling)
    gather_wait(piece(2, 1), 0, 8)
    gather_send(piece(2, 1), 0, 17, sibling)
    gather_wait(piece(2, 1), 1, 9)
    gather_send(piece(2, 1), 1, 18, sibling)

    gather_wait(piece(2, 0, 1), 0, 13)
    gather_wait(piece(2, 0, 1), 1, 14)
    gather_wait(piece(3, 1, 1), None, 15)
    gather_wait(piece(1, 1, 1), None, 16)
    gather_wait(piece(2, 1, 1), 0, 17)
    gather_wait(piece(2, 1, 1), 1, 18)

    last = [piece(2, 0), piece(2, 0, 1), piece(3, 1), piece(3, 1, 1),
            piece(1, 1), piece(1, 1, 1), piece(2, 1), piece(2, 1, 1)]

    x_up, x_down, y_near = in_row_group(1, 0), in_row_group(3, 0), in_row_group(0, 1)

    def finish(dx, dy):
        owner = ((x + dx) % 4) * 2 + (yl + dy) % 2
        span = pl.ds(pl.multiple_of(owner * VP, VP), VP)
        return acc[span, :] + product(owner * 4, 4, last)

    def reduce_send(role, value, device):
        sent[role] = value.astype(jnp.bfloat16)
        remote(sent.at[role], received.at[role], rs_sem.at[role], rr_sem.at[role], device)

    def reduce_wait(role):
        pltpu.make_async_remote_copy(
            src_ref=sent.at[role], dst_ref=received.at[role], send_sem=rs_sem.at[role],
            recv_sem=rr_sem.at[role], device_id=near[0], device_id_type=MESH,
        ).wait_recv()
        return received[role].astype(jnp.float32)

    reduce_send(0, finish(2, 1), x_up)
    reduce_send(1, finish(2, 0), x_down)
    reduce_send(3, finish(3, 1), x_down)
    reduce_send(4, finish(1, 0), x_up)
    partial = finish(1, 1)
    reduce_send(2, partial + reduce_wait(0), x_up)
    partial = finish(3, 0)
    reduce_send(5, partial + reduce_wait(1), x_down)
    span_f = pl.ds(pl.multiple_of((x * 2 + (yl + 1) % 2) * VP, VP), VP)
    span_m = pl.ds(pl.multiple_of(col * VP, VP), VP)
    acc[span_f, :] = finish(0, 1)
    acc[span_m, :] = finish(0, 0)

    total = degree[col]
    for n in range(len(others)):
        pltpu.make_async_remote_copy(
            src_ref=degree.at[0], dst_ref=degree_in.at[n], send_sem=ds_sem.at[n],
            recv_sem=dr_sem.at[n], device_id=near[0], device_id_type=MESH,
        ).wait_recv()
        total = total + degree_in[n]
    factor = lax.rsqrt(1.0 + total)
    diagonal = lax.broadcasted_iota(jnp.int32, (TILE, TILE), 0) == lax.broadcasted_iota(
        jnp.int32, (TILE, TILE), 1
    )
    for q in range(4):
        column = jnp.sum(jnp.where(diagonal, factor[q : q + 1, :], 0.0), axis=1, keepdims=True)
        scale[pl.ds(q * TILE, TILE), :] = jnp.broadcast_to(column, (TILE, TILE))

    reduce_send(6, acc[span_f, :] + reduce_wait(3) + reduce_wait(2), y_near)
    acc[span_m, :] += reduce_wait(4) + reduce_wait(5)
    last_part = reduce_wait(6)
    wide = jnp.concatenate([scale[...], scale[...]], axis=1)
    hidden = (acc[span_m, :] + last_part) * wide + gathered[row].astype(jnp.float32)
    mixed = jnp.dot(hidden.astype(jnp.bfloat16), weight_ref[...], preferred_element_type=jnp.float32)
    out_ref[...] = jnp.maximum(mixed + bias_ref[...], 0.0).astype(jnp.bfloat16)

    for copy in sends:
        copy.wait_send()


def on_device(features, tile_values, tile_index, tile_count, weight, out_bias):
    any_space = pl.BlockSpec(memory_space=pl.ANY)
    vmem = pl.BlockSpec(memory_space=pltpu.VMEM)
    smem = pl.BlockSpec(memory_space=pltpu.SMEM)
    dma = pltpu.SemaphoreType.DMA
    return pl.pallas_call(
        kernel,
        out_shape=jax.ShapeDtypeStruct((VP, F), jnp.bfloat16),
        in_specs=[smem, smem, any_space, any_space, vmem, vmem],
        out_specs=vmem,
        scratch_shapes=[
            pltpu.VMEM((SLOTS + 1, TILE, TILE), jnp.bfloat16),
            pltpu.VMEM((PIECES, VP, F), jnp.bfloat16),
            pltpu.VMEM((OWNERS * VP, F), jnp.float32),
            pltpu.VMEM((N_REDUCE, VP, F), jnp.bfloat16),
            pltpu.VMEM((N_REDUCE, VP, F), jnp.bfloat16),
            pltpu.VMEM((OWNERS, 8, TILE), jnp.float32),
            pltpu.VMEM((OWNERS - 1, 8, TILE), jnp.float32),
            pltpu.VMEM((VP, TILE), jnp.float32),
            pltpu.VMEM((16, TILE), jnp.int32),
            pltpu.SMEM((16, TILE), jnp.int32),
            dma((CHUNKS,)), dma, dma,
            dma((N_GATHER,)), dma((N_GATHER,)),
            dma((N_REDUCE,)), dma((N_REDUCE,)),
            dma((OWNERS - 1,)), dma((OWNERS - 1,)),
        ],
        compiler_params=pltpu.CompilerParams(
            collective_id=1, has_side_effects=True, vmem_limit_bytes=56 * 2**20
        ),
        name="graph_layer",
    )(
        tile_count.reshape(1),
        tile_index.reshape(SLOTS),
        features,
        tile_values.reshape(SLOTS, TILE, TILE),
        weight,
        out_bias.reshape(1, F),
    )


def solution(mesh):
    in_specs = (
        P(("row", "col"), None),
        P("row", "col", None, None, None),
        P("row", "col", None),
        P("row", "col"),
        P(),
        P(),
    )
    return jax.shard_map(
        on_device, mesh=mesh, in_specs=in_specs, out_specs=P(("row", "col"), None), check_vma=False
    )
```

```python
import jax
import jax.numpy as jnp
from jax import lax
from jax.experimental import pallas as pl
from jax.experimental.pallas import tpu as pltpu
from jax.sharding import PartitionSpec as P

TILE = 128
F = 256
VP = 512
HALF = VP // 2
SLOTS = 512
PIECES = 16
OWNERS = 8
CHUNKS = 8
PER_CHUNK = SLOTS // CHUNKS
MESH = pl.DeviceIdType.MESH

GATHER = (
    "own", "below_a", "below_b", "above_a", "above_b", "far_a", "far_b", "two_a", "two_b",
    "far_below_a", "far_below_b", "far_above_a", "far_above_b", "far_two_a", "far_two_b",
    "s_below", "s_above", "s_far", "s_two", "s_far_below", "s_far_above", "s_far_two",
)
REDUCE = (
    "f2_a", "f2_b", "f_up_a", "f_up_b", "f_down_a", "f_down_b", "relay_a", "relay_b",
    "m_up_a", "m_up_b", "m_down_a", "m_down_b", "f_a", "f_b",
)
N_GATHER, N_REDUCE = len(GATHER), len(REDUCE)
EARLY = 4


def kernel(
    count_ref, index_ref, features_ref, values_ref, weight_ref, bias_ref,
    out_ref,
    tiles, gathered, acc, sent, received, degree, degree_in, scale, inverse_v, inverse,
    load_sem, own_sem, inverse_sem, gs_sem, gr_sem, rs_sem, rr_sem, ds_sem, dr_sem,
):
    row = lax.axis_index("row")
    col = lax.axis_index("col")
    z, yh, core = row // 4, (row // 2) % 2, row % 2
    x, yl = col // 2, col % 2

    def owner(dx, dy):
        return ((x + dx) % 4) * 2 + (yl + dy) % 2

    def piece(dz, dy, dk=0):
        return ((z + dz) % 4) * 4 + ((yh + dy) % 2) * 2 + (core + dk) % 2

    def in_row_group(dx, dy):
        return {"row": row, "col": owner(dx, dy)}

    def in_col_group(dz, dy, dk):
        return {"row": piece(dz, dy, dk), "col": col}

    def load(i):
        part = pl.ds(i * PER_CHUNK, PER_CHUNK)
        return pltpu.make_async_copy(values_ref.at[part], tiles.at[part], load_sem.at[i])

    sibling, z_up, z_down, y_far = (
        in_col_group(0, 0, 1), in_col_group(1, 0, 0), in_col_group(3, 0, 0), in_col_group(0, 1, 0)
    )
    x_up, x_down, y_near = in_row_group(1, 0), in_row_group(3, 0), in_row_group(0, 1)
    others = [(dx, dy) for dx in range(4) for dy in range(2) if (dx, dy) != (0, 0)]
    near = [sibling, z_up, z_down, y_far]
    far = [in_row_group(dx, dy) for dx, dy in others]

    barrier = pltpu.get_barrier_semaphore()
    for device in near + far:
        pl.semaphore_signal(barrier, inc=1, device_id=device, device_id_type=MESH)
    for i in range(CHUNKS):
        load(i).start()
    own_copy = pltpu.make_async_copy(features_ref, gathered.at[row], own_sem)
    own_copy.start()

    live = count_ref[0]
    tiles[SLOTS] = jnp.zeros((TILE, TILE), jnp.bfloat16)
    place_id = (
        lax.broadcasted_iota(jnp.int32, (16, TILE), 0) * TILE
        + lax.broadcasted_iota(jnp.int32, (16, TILE), 1)
    )

    def mark(step, found):
        for u in range(16):
            slot = step * 16 + u
            position = jnp.where(slot < live, index_ref[slot], -1)
            found = jnp.where(place_id == position, slot, found)
        return found

    inverse_v[...] = lax.fori_loop(0, SLOTS // 16, mark, jnp.full((16, TILE), SLOTS, jnp.int32))
    inverse_copy = pltpu.make_async_copy(inverse_v, inverse, inverse_sem)
    inverse_copy.start()
    pl.semaphore_wait(barrier, len(near) + len(far))

    halves = {"a": pl.ds(0, HALF), "b": pl.ds(HALF, HALF)}

    def view(which, half):
        return gathered.at[which] if half is None else gathered.at[which, halves[half]]

    gather_sends = []

    def gather_copy(which, half, role, device, own):
        place = view(which, half)
        source = place
        if own:
            source = features_ref if half is None else features_ref.at[halves[half]]
        n = GATHER.index(role)
        return pltpu.make_async_remote_copy(
            src_ref=source, dst_ref=place, send_sem=gs_sem.at[n], recv_sem=gr_sem.at[n],
            device_id=device, device_id_type=MESH,
        )

    def gather_send(which, half, role, device, own=False):
        gather_copy(which, half, role, device, own).start()
        gather_sends.append((half, role))

    def gather_wait(which, half, role):
        gather_copy(which, half, role, sibling, False).wait_recv()

    gather_send(row, "a", "below_a", z_up, True)
    gather_send(row, "b", "above_b", z_down, True)
    gather_send(row, "a", "far_a", y_far, True)
    gather_send(row, "b", "far_b", y_far, True)
    gather_send(row, "b", "below_b", z_up, True)
    gather_send(row, "a", "above_a", z_down, True)
    gather_send(row, None, "own", sibling, True)

    def forward_neighbours():
        gather_wait(piece(3, 0), "a", "below_a")
        gather_send(piece(3, 0), "a", "two_a", z_up)
        gather_wait(piece(1, 0), "b", "above_b")
        gather_send(piece(1, 0), "b", "two_b", z_down)

    def forward_far():
        gather_wait(piece(0, 1), "a", "far_a")
        gather_send(piece(0, 1), "a", "far_below_a", z_up)
        gather_wait(piece(0, 1), "b", "far_b")
        gather_send(piece(0, 1), "b", "far_above_b", z_down)
        gather_wait(piece(3, 0), "b", "below_b")
        gather_send(piece(3, 0), None, "s_below", sibling)
        gather_wait(piece(1, 0), "a", "above_a")
        gather_send(piece(1, 0), None, "s_above", sibling)
        gather_send(piece(0, 1), "b", "far_below_b", z_up)
        gather_send(piece(0, 1), "a", "far_above_a", z_down)
        gather_send(piece(0, 1), None, "s_far", sibling)

    def forward_two():
        gather_wait(piece(2, 0), "a", "two_a")
        gather_send(piece(2, 0), "a", "far_two_a", y_far)
        gather_wait(piece(2, 0), "b", "two_b")
        gather_send(piece(2, 0), "b", "far_two_b", y_far)
        gather_send(piece(2, 0), None, "s_two", sibling)

    def forward_far_below():
        gather_wait(piece(3, 1), "a", "far_below_a")
        gather_wait(piece(3, 1), "b", "far_below_b")
        gather_send(piece(3, 1), None, "s_far_below", sibling)

    def forward_far_above():
        gather_wait(piece(1, 1), "a", "far_above_a")
        gather_wait(piece(1, 1), "b", "far_above_b")
        gather_send(piece(1, 1), None, "s_far_above", sibling)

    def forward_far_two():
        gather_wait(piece(2, 1), "a", "far_two_a")
        gather_wait(piece(2, 1), "b", "far_two_b")
        gather_send(piece(2, 1), None, "s_far_two", sibling)

    row_id = lax.broadcasted_iota(jnp.int32, (OWNERS * 8, TILE), 0)
    degree[...] = jnp.zeros_like(degree)

    def add_degrees(i, _):
        marks, parts = [], []
        for u in range(PER_CHUNK):
            slot = i * PER_CHUNK + u
            tile_row = index_ref[slot] // 64
            at = jnp.where(slot < live, (tile_row // 4) * 8 + tile_row % 4, -1)
            marks.append((row_id == at).astype(jnp.float32).astype(jnp.bfloat16))
            parts.append(tiles[slot])
        sums = lax.dot_general(
            jnp.concatenate(marks, axis=1), jnp.concatenate(parts, axis=1),
            (((1,), (1,)), ((), ())), preferred_element_type=jnp.float32,
        )
        degree[...] += sums.reshape(degree.shape)
        return 0

    def load_and_add(i, _):
        load(i).wait()
        return add_degrees(i, 0)

    acc[...] = jnp.zeros_like(acc)
    lax.fori_loop(0, EARLY, load_and_add, 0)
    for i in range(EARLY, CHUNKS):
        load(i).wait()
    inverse_copy.wait()
    own_copy.wait()

    def product(first_row, rows, pieces):
        half_row = first_row // 2
        lines = []
        for a in range(rows):
            line = []
            for p in pieces:
                for b in range(4):
                    lane = (a % 2) * 64 + p * 4 + b
                    line.append(tiles[inverse[half_row + a // 2, lane]])
            lines.append(jnp.concatenate(line, axis=1))
        sources = jnp.concatenate([gathered[p] for p in pieces], axis=0)
        return jnp.dot(
            jnp.concatenate(lines, axis=0), sources, preferred_element_type=jnp.float32
        )

    def multiply(step, _):
        pair, part = step // 4, step % 4
        dz, dy = ((pair * 3) % 5) % 4, pair // 3
        for at, action in PLAN:
            pl.when(step == at)(action)
        span = pl.ds(pl.multiple_of(part * 8 * TILE, 8 * TILE), 8 * TILE)
        acc[span, :] += product(part * 8, 8, [piece(dz, dy), piece(dz, dy, 1)])
        return 0

    def need(which, role):
        return lambda: gather_wait(piece(*which), None, role)

    def late_degrees():
        lax.fori_loop(EARLY, CHUNKS, add_degrees, 0)

    PLAN = [
        (0, need((0, 0, 1), "own")),
        (2, forward_neighbours),
        (4, forward_far),
        (4, late_degrees),
        (4, need((3, 0, 1), "s_below")),
        (6, forward_two),
        (8, need((1, 0, 1), "s_above")),
        (11, forward_far_below),
        (12, need((0, 1, 1), "s_far")),
        (12, forward_far_above),
        (14, forward_far_two),
    ]
    lax.fori_loop(0, 16, multiply, 0)
    for which, role in (
        ((2, 0, 1), "s_two"), ((3, 1, 1), "s_far_below"), ((1, 1, 1), "s_far_above"),
        ((2, 1, 1), "s_far_two"),
    ):
        gather_wait(piece(*which), None, role)

    last = [piece(dz, dy, dk) for dz, dy in ((2, 0), (3, 1), (1, 1), (2, 1)) for dk in (0, 1)]

    def rows_of(dx, dy, half):
        start = owner(dx, dy) * VP + (HALF if half == "b" else 0)
        return pl.ds(pl.multiple_of(start, HALF), HALF)

    def part(dx, dy, half):
        return acc[rows_of(dx, dy, half), :]

    def reduce_copy(role, device):
        n = REDUCE.index(role)
        return pltpu.make_async_remote_copy(
            src_ref=sent.at[n], dst_ref=received.at[n], send_sem=rs_sem.at[n], recv_sem=rr_sem.at[n],
            device_id=device, device_id_type=MESH,
        )

    def reduce_send(role, value, device):
        sent[REDUCE.index(role)] = value.astype(jnp.bfloat16)
        reduce_copy(role, device).start()

    def reduced(role):
        reduce_copy(role, sibling).wait_recv()
        return received[REDUCE.index(role)].astype(jnp.float32)

    def after_0():
        reduce_send("f2_a", part(2, 1, "a"), y_near)
        reduce_send("f2_b", part(2, 1, "b"), y_near)

    def after_1():
        reduce_send("f_up_a", part(1, 1, "a"), x_up)
        reduce_send("f_up_b", part(1, 1, "b"), x_up)

    def after_2():
        reduce_send("f_down_a", part(3, 1, "a"), x_down)
        reduce_send("f_down_b", part(3, 1, "b"), x_down)

    def after_4():
        reduce_send("m_up_b", part(1, 0, "b"), x_up)
        reduce_send("relay_a", part(2, 0, "a") + reduced("f2_a"), x_up)
        reduce_send("relay_b", part(2, 0, "b") + reduced("f2_b"), x_down)

    def after_5():
        reduce_send("m_down_a", part(3, 0, "a"), x_down)

    def after_6():
        reduce_send("f_a", part(0, 1, "a") + reduced("f_up_a") + reduced("f_down_a"), y_near)
        reduce_send("f_b", part(0, 1, "b") + reduced("f_up_b") + reduced("f_down_b"), y_near)

    def after_7():
        reduce_send("m_up_a", part(1, 0, "a") + reduced("relay_a"), x_up)
        reduce_send("m_down_b", part(3, 0, "b") + reduced("relay_b"), x_down)

    def finish(i, _):
        turn = i % 3
        dx = jnp.where(i >= 6, 0, jnp.where(turn == 0, 2, jnp.where(turn == 1, 1, 3)))
        dy = jnp.where((i < 3) | (i == 6), 1, 0)
        to = owner(dx, dy)
        span = pl.ds(pl.multiple_of(to * VP, VP), VP)
        acc[span, :] += product(to * 4, 4, last)
        for at, action in (
            (0, after_0), (1, after_1), (2, after_2), (4, after_4), (5, after_5), (6, after_6),
            (7, after_7),
        ):
            pl.when(i == at)(action)
        return 0

    def degree_copy(n, dx, dy):
        return pltpu.make_async_remote_copy(
            src_ref=degree.at[owner(dx, dy)], dst_ref=degree_in.at[n], send_sem=ds_sem.at[n],
            recv_sem=dr_sem.at[n], device_id=far[n], device_id_type=MESH,
        )

    for n, (dx, dy) in enumerate(others):
        degree_copy(n, dx, dy).start()
    lax.fori_loop(0, 8, finish, 0)

    total = degree[col]
    for n, (dx, dy) in enumerate(others):
        degree_copy(n, dx, dy).wait_recv()
        total = total + degree_in[n]
    factor = lax.rsqrt(1.0 + total)
    diagonal = lax.broadcasted_iota(jnp.int32, (TILE, TILE), 0) == lax.broadcasted_iota(
        jnp.int32, (TILE, TILE), 1
    )
    for q in range(4):
        column = jnp.sum(jnp.where(diagonal, factor[q : q + 1, :], 0.0), axis=1, keepdims=True)
        scale[pl.ds(q * TILE, TILE), :] = jnp.broadcast_to(column, (TILE, TILE))

    for half in "ab":
        aggregate = part(0, 0, half) + reduced("m_down_" + half) + reduced("m_up_" + half)
        aggregate = aggregate + reduced("f_" + half)
        here = halves[half]
        wide = jnp.concatenate([scale[here, :], scale[here, :]], axis=1)
        hidden = aggregate * wide + gathered[row, here].astype(jnp.float32)
        mixed = jnp.dot(
            hidden.astype(jnp.bfloat16), weight_ref[...], preferred_element_type=jnp.float32
        )
        out_ref[here, :] = jnp.maximum(mixed + bias_ref[...], 0.0).astype(jnp.bfloat16)

    for half, role in gather_sends:
        gather_copy(0, half, role, sibling, False).wait_send()
    for role in REDUCE:
        reduce_copy(role, sibling).wait_send()
    for n, (dx, dy) in enumerate(others):
        degree_copy(n, dx, dy).wait_send()


def on_device(features, tile_values, tile_index, tile_count, weight, out_bias):
    any_space = pl.BlockSpec(memory_space=pl.ANY)
    vmem = pl.BlockSpec(memory_space=pltpu.VMEM)
    smem = pl.BlockSpec(memory_space=pltpu.SMEM)
    dma = pltpu.SemaphoreType.DMA
    return pl.pallas_call(
        kernel,
        out_shape=pltpu.VMEM((VP, F), jnp.bfloat16),
        in_specs=[smem, smem, any_space, any_space, vmem, vmem],
        out_specs=vmem,
        scratch_shapes=[
            pltpu.VMEM((SLOTS + 1, TILE, TILE), jnp.bfloat16),
            pltpu.VMEM((PIECES, VP, F), jnp.bfloat16),
            pltpu.VMEM((OWNERS * VP, F), jnp.float32),
            pltpu.VMEM((N_REDUCE, HALF, F), jnp.bfloat16),
            pltpu.VMEM((N_REDUCE, HALF, F), jnp.bfloat16),
            pltpu.VMEM((OWNERS, 8, TILE), jnp.float32),
            pltpu.VMEM((OWNERS - 1, 8, TILE), jnp.float32),
            pltpu.VMEM((VP, TILE), jnp.float32),
            pltpu.VMEM((16, TILE), jnp.int32),
            pltpu.SMEM((16, TILE), jnp.int32),
            dma((CHUNKS,)), dma, dma,
            dma((N_GATHER,)), dma((N_GATHER,)),
            dma((N_REDUCE,)), dma((N_REDUCE,)),
            dma((OWNERS - 1,)), dma((OWNERS - 1,)),
        ],
        compiler_params=pltpu.CompilerParams(
            collective_id=1, has_side_effects=True, vmem_limit_bytes=56 * 2**20
        ),
        name="graph_layer",
    )(
        tile_count.reshape(1),
        tile_index.reshape(SLOTS),
        features,
        tile_values.reshape(SLOTS, TILE, TILE),
        weight,
        out_bias.reshape(1, F),
    )


def solution(mesh):
    in_specs = (
        P(("row", "col"), None),
        P("row", "col", None, None, None),
        P("row", "col", None),
        P("row", "col"),
        P(),
        P(),
    )
    return jax.shard_map(
        on_device, mesh=mesh, in_specs=in_specs, out_specs=P(("row", "col"), None), check_vma=False
    )
```

```python
import jax
import jax.numpy as jnp
from jax import lax
from jax.experimental import pallas as pl
from jax.experimental.pallas import tpu as pltpu
from jax.sharding import PartitionSpec as P

TILE = 128
F = 256
VP = 512
HALF = VP // 2
SLOTS = 512
PIECES = 16
OWNERS = 8
CHUNKS = 8
PER_CHUNK = SLOTS // CHUNKS
MESH = pl.DeviceIdType.MESH

GATHER = (
    "own", "below_a", "below_b", "above_a", "above_b", "far_a", "far_b", "two_a", "two_b",
    "far_below_a", "far_below_b", "far_above_a", "far_above_b", "far_two_a", "far_two_b",
    "s_below", "s_above", "s_far", "s_two", "s_far_below", "s_far_above", "s_far_two",
)
REDUCE = (
    "f2_a", "f2_b", "f_up_a", "f_up_b", "f_down_a", "f_down_b", "relay_a", "relay_b",
    "m_up_a", "m_up_b", "m_down_a", "m_down_b", "f_a", "f_b",
)
N_GATHER, N_REDUCE = len(GATHER), len(REDUCE)
EARLY = 5


def kernel(
    count_ref, index_ref, features_ref, values_ref, weight_ref, bias_ref,
    out_ref,
    tiles, gathered, acc, sent, received, degree, degree_in, scale, inverse_v, inverse,
    load_sem, own_sem, inverse_sem, gs_sem, gr_sem, rs_sem, rr_sem, ds_sem, dr_sem,
):
    row = lax.axis_index("row")
    col = lax.axis_index("col")
    z, yh, core = row // 4, (row // 2) % 2, row % 2
    x, yl = col // 2, col % 2

    def owner(dx, dy):
        return ((x + dx) % 4) * 2 + (yl + dy) % 2

    def piece(dz, dy, dk=0):
        return ((z + dz) % 4) * 4 + ((yh + dy) % 2) * 2 + (core + dk) % 2

    def in_row_group(dx, dy):
        return {"row": row, "col": owner(dx, dy)}

    def in_col_group(dz, dy, dk):
        return {"row": piece(dz, dy, dk), "col": col}

    def load(i):
        part = pl.ds(i * PER_CHUNK, PER_CHUNK)
        return pltpu.make_async_copy(values_ref.at[part], tiles.at[part], load_sem.at[i])

    sibling, z_up, z_down, y_far = (
        in_col_group(0, 0, 1), in_col_group(1, 0, 0), in_col_group(3, 0, 0), in_col_group(0, 1, 0)
    )
    x_up, x_down, y_near = in_row_group(1, 0), in_row_group(3, 0), in_row_group(0, 1)
    others = [(dx, dy) for dx in range(4) for dy in range(2) if (dx, dy) != (0, 0)]
    near = [sibling, z_up, z_down, y_far]
    far = [in_row_group(dx, dy) for dx, dy in others]

    barrier = pltpu.get_barrier_semaphore()
    for device in near + far:
        pl.semaphore_signal(barrier, inc=1, device_id=device, device_id_type=MESH)
    for i in range(CHUNKS):
        load(i).start()
    own_copy = pltpu.make_async_copy(features_ref, gathered.at[row], own_sem)
    own_copy.start()

    live = count_ref[0]
    tiles[SLOTS] = jnp.zeros((TILE, TILE), jnp.bfloat16)
    place_id = (
        lax.broadcasted_iota(jnp.int32, (16, TILE), 0) * TILE
        + lax.broadcasted_iota(jnp.int32, (16, TILE), 1)
    )

    def mark(step, found):
        for u in range(16):
            slot = step * 16 + u
            position = jnp.where(slot < live, index_ref[slot], -1)
            found = jnp.where(place_id == position, slot, found)
        return found

    inverse_v[...] = lax.fori_loop(0, SLOTS // 16, mark, jnp.full((16, TILE), SLOTS, jnp.int32))
    inverse_copy = pltpu.make_async_copy(inverse_v, inverse, inverse_sem)
    inverse_copy.start()
    pl.semaphore_wait(barrier, len(near) + len(far))

    halves = {"a": pl.ds(0, HALF), "b": pl.ds(HALF, HALF)}

    def view(which, half):
        return gathered.at[which] if half is None else gathered.at[which, halves[half]]

    gather_sends = []

    def gather_copy(which, half, role, device, own):
        place = view(which, half)
        source = place
        if own:
            source = features_ref if half is None else features_ref.at[halves[half]]
        n = GATHER.index(role)
        return pltpu.make_async_remote_copy(
            src_ref=source, dst_ref=place, send_sem=gs_sem.at[n], recv_sem=gr_sem.at[n],
            device_id=device, device_id_type=MESH,
        )

    def gather_send(which, half, role, device, own=False):
        gather_copy(which, half, role, device, own).start()
        gather_sends.append((half, role))

    def gather_wait(which, half, role):
        gather_copy(which, half, role, sibling, False).wait_recv()

    gather_send(row, "a", "below_a", z_up, True)
    gather_send(row, "b", "above_b", z_down, True)
    gather_send(row, "a", "far_a", y_far, True)
    gather_send(row, "b", "far_b", y_far, True)
    gather_send(row, "b", "below_b", z_up, True)
    gather_send(row, "a", "above_a", z_down, True)
    gather_send(row, None, "own", sibling, True)

    def forward_neighbours():
        gather_wait(piece(3, 0), "a", "below_a")
        gather_send(piece(3, 0), "a", "two_a", z_up)
        gather_wait(piece(1, 0), "b", "above_b")
        gather_send(piece(1, 0), "b", "two_b", z_down)

    def forward_far():
        gather_wait(piece(0, 1), "a", "far_a")
        gather_send(piece(0, 1), "a", "far_below_a", z_up)
        gather_wait(piece(0, 1), "b", "far_b")
        gather_send(piece(0, 1), "b", "far_above_b", z_down)
        gather_wait(piece(3, 0), "b", "below_b")
        gather_send(piece(3, 0), None, "s_below", sibling)
        gather_wait(piece(1, 0), "a", "above_a")
        gather_send(piece(1, 0), None, "s_above", sibling)
        gather_send(piece(0, 1), "b", "far_below_b", z_up)
        gather_send(piece(0, 1), "a", "far_above_a", z_down)
        gather_send(piece(0, 1), None, "s_far", sibling)

    def forward_two():
        gather_wait(piece(2, 0), "a", "two_a")
        gather_send(piece(2, 0), "a", "far_two_a", y_far)
        gather_wait(piece(2, 0), "b", "two_b")
        gather_send(piece(2, 0), "b", "far_two_b", y_far)
        gather_send(piece(2, 0), None, "s_two", sibling)

    def forward_far_below():
        gather_wait(piece(3, 1), "a", "far_below_a")
        gather_wait(piece(3, 1), "b", "far_below_b")
        gather_send(piece(3, 1), None, "s_far_below", sibling)

    def forward_far_above():
        gather_wait(piece(1, 1), "a", "far_above_a")
        gather_wait(piece(1, 1), "b", "far_above_b")
        gather_send(piece(1, 1), None, "s_far_above", sibling)

    def forward_far_two():
        gather_wait(piece(2, 1), "a", "far_two_a")
        gather_wait(piece(2, 1), "b", "far_two_b")
        gather_send(piece(2, 1), None, "s_far_two", sibling)

    row_id = lax.broadcasted_iota(jnp.int32, (OWNERS * 8, TILE), 0)
    degree[...] = jnp.zeros_like(degree)

    def add_degrees(i, _):
        marks, parts = [], []
        for u in range(PER_CHUNK):
            slot = i * PER_CHUNK + u
            tile_row = index_ref[slot] // 64
            at = jnp.where(slot < live, (tile_row // 4) * 8 + tile_row % 4, -1)
            marks.append((row_id == at).astype(jnp.float32).astype(jnp.bfloat16))
            parts.append(tiles[slot])
        sums = lax.dot_general(
            jnp.concatenate(marks, axis=1), jnp.concatenate(parts, axis=1),
            (((1,), (1,)), ((), ())), preferred_element_type=jnp.float32,
        )
        degree[...] += sums.reshape(degree.shape)
        return 0

    def load_and_add(i, _):
        load(i).wait()
        return add_degrees(i, 0)

    acc[...] = jnp.zeros_like(acc)
    lax.fori_loop(0, EARLY, load_and_add, 0)
    for i in range(EARLY, CHUNKS):
        load(i).wait()
    inverse_copy.wait()
    own_copy.wait()

    def product(first_row, rows, pieces):
        half_row = first_row // 2
        lines = []
        for a in range(rows):
            line = []
            for p in pieces:
                for b in range(4):
                    lane = (a % 2) * 64 + p * 4 + b
                    line.append(tiles[inverse[half_row + a // 2, lane]])
            lines.append(jnp.concatenate(line, axis=1))
        sources = jnp.concatenate([gathered[p] for p in pieces], axis=0)
        return jnp.dot(
            jnp.concatenate(lines, axis=0), sources, preferred_element_type=jnp.float32
        )

    def multiply(step, _):
        pair, part = step // 4, step % 4
        dz, dy = ((pair * 3) % 5) % 4, pair // 3
        for at, action in PLAN:
            pl.when(step == at)(action)
        span = pl.ds(pl.multiple_of(part * 8 * TILE, 8 * TILE), 8 * TILE)
        acc[span, :] += product(part * 8, 8, [piece(dz, dy), piece(dz, dy, 1)])
        return 0

    def need(which, role):
        return lambda: gather_wait(piece(*which), None, role)

    def late_degrees():
        lax.fori_loop(EARLY, CHUNKS, add_degrees, 0)

    PLAN = [
        (0, need((0, 0, 1), "own")),
        (1, forward_neighbours),
        (4, forward_far),
        (4, late_degrees),
        (4, forward_two),
        (4, need((3, 0, 1), "s_below")),
        (8, need((1, 0, 1), "s_above")),
        (10, forward_far_below),
        (11, forward_far_above),
        (12, need((0, 1, 1), "s_far")),
        (13, forward_far_two),
    ]
    lax.fori_loop(0, 16, multiply, 0)
    for which, role in (
        ((2, 0, 1), "s_two"), ((3, 1, 1), "s_far_below"), ((1, 1, 1), "s_far_above"),
        ((2, 1, 1), "s_far_two"),
    ):
        gather_wait(piece(*which), None, role)

    last = [piece(dz, dy, dk) for dz, dy in ((2, 0), (3, 1), (1, 1), (2, 1)) for dk in (0, 1)]

    def rows_of(dx, dy, half):
        start = owner(dx, dy) * VP + (HALF if half == "b" else 0)
        return pl.ds(pl.multiple_of(start, HALF), HALF)

    def part(dx, dy, half):
        return acc[rows_of(dx, dy, half), :]

    def reduce_copy(role, device):
        n = REDUCE.index(role)
        return pltpu.make_async_remote_copy(
            src_ref=sent.at[n], dst_ref=received.at[n], send_sem=rs_sem.at[n], recv_sem=rr_sem.at[n],
            device_id=device, device_id_type=MESH,
        )

    def reduce_send(role, value, device):
        sent[REDUCE.index(role)] = value.astype(jnp.bfloat16)
        reduce_copy(role, device).start()

    def reduced(role):
        reduce_copy(role, sibling).wait_recv()
        return received[REDUCE.index(role)].astype(jnp.float32)

    def after_0():
        reduce_send("f2_a", part(2, 1, "a"), y_near)

    def after_1():
        reduce_send("f2_b", part(2, 1, "b"), y_near)
        reduce_send("f_up_a", part(1, 1, "a"), x_up)

    def after_2():
        reduce_send("f_up_b", part(1, 1, "b"), x_up)
        reduce_send("f_down_a", part(3, 1, "a"), x_down)

    def after_3():
        reduce_send("f_down_b", part(3, 1, "b"), y_near)
        reduce_send("relay_a", part(2, 0, "a") + reduced("f2_a"), x_up)

    def after_4():
        reduce_send("relay_b", part(2, 0, "b") + reduced("f2_b"), x_down)

    def after_5():
        reduce_send("f_a", part(0, 1, "a") + reduced("f_up_a") + reduced("f_down_a"), y_near)
        reduce_send("m_up_b", part(1, 0, "b"), x_up)

    def after_6():
        reduce_send("f_b", part(0, 1, "b") + reduced("f_up_b"), y_near)
        reduce_send("m_down_a", part(3, 0, "a"), x_down)

    def after_7():
        reduce_send("m_up_a", part(1, 0, "a") + reduced("relay_a"), x_up)
        reduce_send("m_down_b", part(3, 0, "b") + reduced("relay_b") + reduced("f_down_b"), x_down)

    def finish(i, _):
        dx = jnp.where((i == 0) | (i == 3), 2, jnp.where((i == 1) | (i == 5), 1, jnp.where((i == 2) | (i == 6), 3, 0)))
        dy = jnp.where((i < 3) | (i == 4), 1, 0)
        to = owner(dx, dy)
        span = pl.ds(pl.multiple_of(to * VP, VP), VP)
        acc[span, :] += product(to * 4, 4, last)
        for at, action in (
            (0, after_0), (1, after_1), (2, after_2), (3, after_3), (4, after_4), (5, after_5),
            (6, after_6), (7, after_7),
        ):
            pl.when(i == at)(action)
        return 0

    def degree_copy(n, dx, dy):
        return pltpu.make_async_remote_copy(
            src_ref=degree.at[owner(dx, dy)], dst_ref=degree_in.at[n], send_sem=ds_sem.at[n],
            recv_sem=dr_sem.at[n], device_id=far[n], device_id_type=MESH,
        )

    for n, (dx, dy) in enumerate(others):
        degree_copy(n, dx, dy).start()
    lax.fori_loop(0, 8, finish, 0)

    total = degree[col]
    for n, (dx, dy) in enumerate(others):
        degree_copy(n, dx, dy).wait_recv()
        total = total + degree_in[n]
    factor = lax.rsqrt(1.0 + total)
    diagonal = lax.broadcasted_iota(jnp.int32, (TILE, TILE), 0) == lax.broadcasted_iota(
        jnp.int32, (TILE, TILE), 1
    )
    for q in range(4):
        column = jnp.sum(jnp.where(diagonal, factor[q : q + 1, :], 0.0), axis=1, keepdims=True)
        scale[pl.ds(q * TILE, TILE), :] = jnp.broadcast_to(column, (TILE, TILE))

    for half in "ab":
        aggregate = part(0, 0, half) + reduced("m_down_" + half) + reduced("m_up_" + half)
        aggregate = aggregate + reduced("f_" + half)
        here = halves[half]
        wide = jnp.concatenate([scale[here, :], scale[here, :]], axis=1)
        hidden = aggregate * wide + gathered[row, here].astype(jnp.float32)
        mixed = jnp.dot(
            hidden.astype(jnp.bfloat16), weight_ref[...], preferred_element_type=jnp.float32
        )
        out_ref[here, :] = jnp.maximum(mixed + bias_ref[...], 0.0).astype(jnp.bfloat16)

    for half, role in gather_sends:
        gather_copy(0, half, role, sibling, False).wait_send()
    for role in REDUCE:
        reduce_copy(role, sibling).wait_send()
    for n, (dx, dy) in enumerate(others):
        degree_copy(n, dx, dy).wait_send()


def on_device(features, tile_values, tile_index, tile_count, weight, out_bias):
    any_space = pl.BlockSpec(memory_space=pl.ANY)
    vmem = pl.BlockSpec(memory_space=pltpu.VMEM)
    smem = pl.BlockSpec(memory_space=pltpu.SMEM)
    dma = pltpu.SemaphoreType.DMA
    return pl.pallas_call(
        kernel,
        out_shape=pltpu.VMEM((VP, F), jnp.bfloat16),
        in_specs=[smem, smem, any_space, any_space, vmem, vmem],
        out_specs=vmem,
        scratch_shapes=[
            pltpu.VMEM((SLOTS + 1, TILE, TILE), jnp.bfloat16),
            pltpu.VMEM((PIECES, VP, F), jnp.bfloat16),
            pltpu.VMEM((OWNERS * VP, F), jnp.float32),
            pltpu.VMEM((N_REDUCE, HALF, F), jnp.bfloat16),
            pltpu.VMEM((N_REDUCE, HALF, F), jnp.bfloat16),
            pltpu.VMEM((OWNERS, 8, TILE), jnp.float32),
            pltpu.VMEM((OWNERS - 1, 8, TILE), jnp.float32),
            pltpu.VMEM((VP, TILE), jnp.float32),
            pltpu.VMEM((16, TILE), jnp.int32),
            pltpu.SMEM((16, TILE), jnp.int32),
            dma((CHUNKS,)), dma, dma,
            dma((N_GATHER,)), dma((N_GATHER,)),
            dma((N_REDUCE,)), dma((N_REDUCE,)),
            dma((OWNERS - 1,)), dma((OWNERS - 1,)),
        ],
        compiler_params=pltpu.CompilerParams(
            collective_id=1, has_side_effects=True, vmem_limit_bytes=56 * 2**20
        ),
        name="graph_layer",
    )(
        tile_count.reshape(1),
        tile_index.reshape(SLOTS),
        features,
        tile_values.reshape(SLOTS, TILE, TILE),
        weight,
        out_bias.reshape(1, F),
    )


def solution(mesh):
    in_specs = (
        P(("row", "col"), None),
        P("row", "col", None, None, None),
        P("row", "col", None),
        P("row", "col"),
        P(),
        P(),
    )
    return jax.shard_map(
        on_device, mesh=mesh, in_specs=in_specs, out_specs=P(("row", "col"), None), check_vma=False
    )
```

```python
import jax
import jax.numpy as jnp
from jax import lax
from jax.experimental import pallas as pl
from jax.experimental.pallas import tpu as pltpu
from jax.sharding import PartitionSpec as P

TILE = 128
F = 256
VP = 512
HALF = VP // 2
SLOTS = 512
PIECES = 16
OWNERS = 8
CHUNKS = 8
PER_CHUNK = SLOTS // CHUNKS
MESH = pl.DeviceIdType.MESH

GATHER = (
    "own", "below_a", "below_b", "above_a", "above_b", "far_a", "far_b", "two_a", "two_b",
    "far_below_a", "far_below_b", "far_above_a", "far_above_b", "far_two_a", "far_two_b",
    "s_below", "s_above", "s_far", "s_two", "s_far_below", "s_far_above", "s_far_two",
)
REDUCE = (
    "f2_a", "f2_b", "f_up_a", "f_up_b", "f_down_a", "f_down_b", "relay_a", "relay_b",
    "m_up_a", "m_up_b", "m_down_a", "m_down_b", "f_a", "f_b",
)
N_GATHER, N_REDUCE = len(GATHER), len(REDUCE)
EARLY = 5


def kernel(
    count_ref, index_ref, features_ref, values_ref, weight_ref, bias_ref,
    out_ref,
    tiles, gathered, acc, sent, received, degree, degree_in, scale, inverse_v, inverse,
    load_sem, own_sem, inverse_sem, gs_sem, gr_sem, rs_sem, rr_sem, ds_sem, dr_sem,
):
    row = lax.axis_index("row")
    col = lax.axis_index("col")
    z, yh, core = row // 4, (row // 2) % 2, row % 2
    x, yl = col // 2, col % 2

    def owner(dx, dy):
        return ((x + dx) % 4) * 2 + (yl + dy) % 2

    def piece(dz, dy, dk=0):
        return ((z + dz) % 4) * 4 + ((yh + dy) % 2) * 2 + (core + dk) % 2

    def in_row_group(dx, dy):
        return {"row": row, "col": owner(dx, dy)}

    def in_col_group(dz, dy, dk):
        return {"row": piece(dz, dy, dk), "col": col}

    def load(i):
        part = pl.ds(i * PER_CHUNK, PER_CHUNK)
        return pltpu.make_async_copy(values_ref.at[part], tiles.at[part], load_sem.at[i])

    sibling, z_up, z_down, y_far = (
        in_col_group(0, 0, 1), in_col_group(1, 0, 0), in_col_group(3, 0, 0), in_col_group(0, 1, 0)
    )
    x_up, x_down, y_near = in_row_group(1, 0), in_row_group(3, 0), in_row_group(0, 1)
    others = [(dx, dy) for dx in range(4) for dy in range(2) if (dx, dy) != (0, 0)]
    near = [sibling, z_up, z_down, y_far]
    far = [in_row_group(dx, dy) for dx, dy in others]

    barrier = pltpu.get_barrier_semaphore()
    for device in near + far:
        pl.semaphore_signal(barrier, inc=1, device_id=device, device_id_type=MESH)
    for i in range(CHUNKS):
        load(i).start()
    own_copy = pltpu.make_async_copy(features_ref, gathered.at[row], own_sem)
    own_copy.start()

    live = count_ref[0]
    tiles[SLOTS] = jnp.zeros((TILE, TILE), jnp.bfloat16)
    place_id = (
        lax.broadcasted_iota(jnp.int32, (16, TILE), 0) * TILE
        + lax.broadcasted_iota(jnp.int32, (16, TILE), 1)
    )

    def mark(step, found):
        for u in range(16):
            slot = step * 16 + u
            position = jnp.where(slot < live, index_ref[slot], -1)
            found = jnp.where(place_id == position, slot, found)
        return found

    inverse_v[...] = lax.fori_loop(0, SLOTS // 16, mark, jnp.full((16, TILE), SLOTS, jnp.int32))
    inverse_copy = pltpu.make_async_copy(inverse_v, inverse, inverse_sem)
    inverse_copy.start()
    pl.semaphore_wait(barrier, len(near) + len(far))

    halves = {"a": pl.ds(0, HALF), "b": pl.ds(HALF, HALF)}

    def view(which, half):
        return gathered.at[which] if half is None else gathered.at[which, halves[half]]

    gather_sends = []

    def gather_copy(which, half, role, device, own):
        place = view(which, half)
        source = place
        if own:
            source = features_ref if half is None else features_ref.at[halves[half]]
        n = GATHER.index(role)
        return pltpu.make_async_remote_copy(
            src_ref=source, dst_ref=place, send_sem=gs_sem.at[n], recv_sem=gr_sem.at[n],
            device_id=device, device_id_type=MESH,
        )

    def gather_send(which, half, role, device, own=False):
        gather_copy(which, half, role, device, own).start()
        gather_sends.append((half, role))

    def gather_wait(which, half, role):
        gather_copy(which, half, role, sibling, False).wait_recv()

    gather_send(row, "a", "below_a", z_up, True)
    gather_send(row, "b", "above_b", z_down, True)
    gather_send(row, "a", "far_a", y_far, True)
    gather_send(row, "b", "far_b", y_far, True)
    gather_send(row, "b", "below_b", z_up, True)
    gather_send(row, "a", "above_a", z_down, True)
    gather_send(row, None, "own", sibling, True)

    def forward_neighbours():
        gather_wait(piece(3, 0), "a", "below_a")
        gather_send(piece(3, 0), "a", "two_a", z_up)
        gather_wait(piece(1, 0), "b", "above_b")
        gather_send(piece(1, 0), "b", "two_b", z_down)

    def forward_far():
        gather_wait(piece(0, 1), "a", "far_a")
        gather_send(piece(0, 1), "a", "far_below_a", z_up)
        gather_wait(piece(0, 1), "b", "far_b")
        gather_send(piece(0, 1), "b", "far_above_b", z_down)
        gather_wait(piece(3, 0), "b", "below_b")
        gather_send(piece(3, 0), None, "s_below", sibling)
        gather_wait(piece(1, 0), "a", "above_a")
        gather_send(piece(1, 0), None, "s_above", sibling)
        gather_send(piece(0, 1), "b", "far_below_b", z_up)
        gather_send(piece(0, 1), "a", "far_above_a", z_down)
        gather_send(piece(0, 1), None, "s_far", sibling)

    def forward_two():
        gather_wait(piece(2, 0), "a", "two_a")
        gather_send(piece(2, 0), "a", "far_two_a", y_far)
        gather_wait(piece(2, 0), "b", "two_b")
        gather_send(piece(2, 0), "b", "far_two_b", y_far)
        gather_send(piece(2, 0), None, "s_two", sibling)

    def forward_far_below():
        gather_wait(piece(3, 1), "a", "far_below_a")
        gather_wait(piece(3, 1), "b", "far_below_b")
        gather_send(piece(3, 1), None, "s_far_below", sibling)

    def forward_far_above():
        gather_wait(piece(1, 1), "a", "far_above_a")
        gather_wait(piece(1, 1), "b", "far_above_b")
        gather_send(piece(1, 1), None, "s_far_above", sibling)

    def forward_far_two():
        gather_wait(piece(2, 1), "a", "far_two_a")
        gather_wait(piece(2, 1), "b", "far_two_b")
        gather_send(piece(2, 1), None, "s_far_two", sibling)

    row_id = lax.broadcasted_iota(jnp.int32, (OWNERS * 8, TILE), 0)
    degree[...] = jnp.zeros_like(degree)

    def add_degrees(i, _):
        marks, parts = [], []
        for u in range(PER_CHUNK):
            slot = i * PER_CHUNK + u
            tile_row = index_ref[slot] // 64
            at = jnp.where(slot < live, (tile_row // 4) * 8 + tile_row % 4, -1)
            marks.append((row_id == at).astype(jnp.float32).astype(jnp.bfloat16))
            parts.append(tiles[slot])
        sums = lax.dot_general(
            jnp.concatenate(marks, axis=1), jnp.concatenate(parts, axis=1),
            (((1,), (1,)), ((), ())), preferred_element_type=jnp.float32,
        )
        degree[...] += sums.reshape(degree.shape)
        return 0

    def load_and_add(i, _):
        load(i).wait()
        return add_degrees(i, 0)

    acc[...] = jnp.zeros_like(acc)
    lax.fori_loop(0, EARLY, load_and_add, 0)
    for i in range(EARLY, CHUNKS):
        load(i).wait()
    inverse_copy.wait()
    own_copy.wait()

    def product(first_row, rows, pieces):
        half_row = first_row // 2
        lines = []
        for a in range(rows):
            line = []
            for p in pieces:
                for b in range(4):
                    lane = (a % 2) * 64 + p * 4 + b
                    line.append(tiles[inverse[half_row + a // 2, lane]])
            lines.append(jnp.concatenate(line, axis=1))
        sources = jnp.concatenate([gathered[p] for p in pieces], axis=0)
        return jnp.dot(
            jnp.concatenate(lines, axis=0), sources, preferred_element_type=jnp.float32
        )

    def multiply(pairs, plan):
        pieces = [piece(dz, dy, dk) for dz, dy in pairs for dk in (0, 1)]

        def step(part, _):
            for at, action in plan:
                pl.when(part == at)(action)
            span = pl.ds(pl.multiple_of(part * 8 * TILE, 8 * TILE), 8 * TILE)
            acc[span, :] += product(part * 8, 8, pieces)
            return 0

        lax.fori_loop(0, 4, step, 0)

    def need(which, role):
        return lambda: gather_wait(piece(*which), None, role)

    def late_degrees():
        lax.fori_loop(EARLY, CHUNKS, add_degrees, 0)

    multiply([(0, 0)], [
        (0, need((0, 0, 1), "own")),
        (1, forward_neighbours),
    ])
    multiply([(3, 0)], [
        (0, forward_far),
        (0, late_degrees),
        (0, need((3, 0, 1), "s_below")),
        (0, forward_two),
    ])
    multiply([(1, 0)], [
        (0, need((1, 0, 1), "s_above")),
        (2, forward_far_below),
        (3, forward_far_above),
    ])
    multiply([(0, 1)], [
        (0, need((0, 1, 1), "s_far")),
        (1, forward_far_two),
    ])
    for which, role in (
        ((2, 0, 1), "s_two"), ((3, 1, 1), "s_far_below"), ((1, 1, 1), "s_far_above"),
        ((2, 1, 1), "s_far_two"),
    ):
        gather_wait(piece(*which), None, role)

    last = [piece(dz, dy, dk) for dz, dy in ((2, 0), (3, 1), (1, 1), (2, 1)) for dk in (0, 1)]

    def rows_of(dx, dy, half):
        start = owner(dx, dy) * VP + (HALF if half == "b" else 0)
        return pl.ds(pl.multiple_of(start, HALF), HALF)

    def part(dx, dy, half):
        return acc[rows_of(dx, dy, half), :]

    def reduce_copy(role, device):
        n = REDUCE.index(role)
        return pltpu.make_async_remote_copy(
            src_ref=sent.at[n], dst_ref=received.at[n], send_sem=rs_sem.at[n], recv_sem=rr_sem.at[n],
            device_id=device, device_id_type=MESH,
        )

    def reduce_send(role, value, device):
        sent[REDUCE.index(role)] = value.astype(jnp.bfloat16)
        reduce_copy(role, device).start()

    def reduced(role):
        reduce_copy(role, sibling).wait_recv()
        return received[REDUCE.index(role)].astype(jnp.float32)

    def after_0():
        reduce_send("f2_a", part(2, 1, "a"), y_near)

    def after_1():
        reduce_send("f2_b", part(2, 1, "b"), y_near)
        reduce_send("f_up_a", part(1, 1, "a"), x_up)

    def after_2():
        reduce_send("f_up_b", part(1, 1, "b"), x_up)
        reduce_send("f_down_a", part(3, 1, "a"), x_down)

    def after_3():
        reduce_send("f_down_b", part(3, 1, "b"), y_near)
        reduce_send("relay_a", part(2, 0, "a") + reduced("f2_a"), x_up)

    def after_4():
        reduce_send("relay_b", part(2, 0, "b") + reduced("f2_b"), x_down)

    def after_5():
        reduce_send("f_a", part(0, 1, "a") + reduced("f_up_a") + reduced("f_down_a"), y_near)
        reduce_send("m_up_b", part(1, 0, "b"), x_up)

    def after_6():
        reduce_send("f_b", part(0, 1, "b") + reduced("f_up_b"), y_near)
        reduce_send("m_down_a", part(3, 0, "a"), x_down)

    def after_7():
        reduce_send("m_up_a", part(1, 0, "a") + reduced("relay_a"), x_up)
        reduce_send("m_down_b", part(3, 0, "b") + reduced("relay_b") + reduced("f_down_b"), x_down)

    def finish(i, _):
        dx = jnp.where((i == 0) | (i == 3), 2, jnp.where((i == 1) | (i == 5), 1, jnp.where((i == 2) | (i == 6), 3, 0)))
        dy = jnp.where((i < 3) | (i == 4), 1, 0)
        to = owner(dx, dy)
        span = pl.ds(pl.multiple_of(to * VP, VP), VP)
        acc[span, :] += product(to * 4, 4, last)
        for at, action in (
            (0, after_0), (1, after_1), (2, after_2), (3, after_3), (4, after_4), (5, after_5),
            (6, after_6), (7, after_7),
        ):
            pl.when(i == at)(action)
        return 0

    def degree_copy(n, dx, dy):
        return pltpu.make_async_remote_copy(
            src_ref=degree.at[owner(dx, dy)], dst_ref=degree_in.at[n], send_sem=ds_sem.at[n],
            recv_sem=dr_sem.at[n], device_id=far[n], device_id_type=MESH,
        )

    for n, (dx, dy) in enumerate(others):
        degree_copy(n, dx, dy).start()
    lax.fori_loop(0, 8, finish, 0)

    total = degree[col]
    for n, (dx, dy) in enumerate(others):
        degree_copy(n, dx, dy).wait_recv()
        total = total + degree_in[n]
    factor = lax.rsqrt(1.0 + total)
    diagonal = lax.broadcasted_iota(jnp.int32, (TILE, TILE), 0) == lax.broadcasted_iota(
        jnp.int32, (TILE, TILE), 1
    )
    for q in range(4):
        column = jnp.sum(jnp.where(diagonal, factor[q : q + 1, :], 0.0), axis=1, keepdims=True)
        scale[pl.ds(q * TILE, TILE), :] = jnp.broadcast_to(column, (TILE, TILE))

    for half in "ab":
        aggregate = part(0, 0, half) + reduced("m_down_" + half) + reduced("m_up_" + half)
        aggregate = aggregate + reduced("f_" + half)
        here = halves[half]
        wide = jnp.concatenate([scale[here, :], scale[here, :]], axis=1)
        hidden = aggregate * wide + gathered[row, here].astype(jnp.float32)
        mixed = jnp.dot(
            hidden.astype(jnp.bfloat16), weight_ref[...], preferred_element_type=jnp.float32
        )
        out_ref[here, :] = jnp.maximum(mixed + bias_ref[...], 0.0).astype(jnp.bfloat16)

    for half, role in gather_sends:
        gather_copy(0, half, role, sibling, False).wait_send()
    for role in REDUCE:
        reduce_copy(role, sibling).wait_send()
    for n, (dx, dy) in enumerate(others):
        degree_copy(n, dx, dy).wait_send()


def on_device(features, tile_values, tile_index, tile_count, weight, out_bias):
    any_space = pl.BlockSpec(memory_space=pl.ANY)
    vmem = pl.BlockSpec(memory_space=pltpu.VMEM)
    smem = pl.BlockSpec(memory_space=pltpu.SMEM)
    dma = pltpu.SemaphoreType.DMA
    return pl.pallas_call(
        kernel,
        out_shape=pltpu.VMEM((VP, F), jnp.bfloat16),
        in_specs=[smem, smem, any_space, any_space, vmem, vmem],
        out_specs=vmem,
        scratch_shapes=[
            pltpu.VMEM((SLOTS + 1, TILE, TILE), jnp.bfloat16),
            pltpu.VMEM((PIECES, VP, F), jnp.bfloat16),
            pltpu.VMEM((OWNERS * VP, F), jnp.float32),
            pltpu.VMEM((N_REDUCE, HALF, F), jnp.bfloat16),
            pltpu.VMEM((N_REDUCE, HALF, F), jnp.bfloat16),
            pltpu.VMEM((OWNERS, 8, TILE), jnp.float32),
            pltpu.VMEM((OWNERS - 1, 8, TILE), jnp.float32),
            pltpu.VMEM((VP, TILE), jnp.float32),
            pltpu.VMEM((16, TILE), jnp.int32),
            pltpu.SMEM((16, TILE), jnp.int32),
            dma((CHUNKS,)), dma, dma,
            dma((N_GATHER,)), dma((N_GATHER,)),
            dma((N_REDUCE,)), dma((N_REDUCE,)),
            dma((OWNERS - 1,)), dma((OWNERS - 1,)),
        ],
        compiler_params=pltpu.CompilerParams(
            collective_id=1, has_side_effects=True, vmem_limit_bytes=56 * 2**20
        ),
        name="graph_layer",
    )(
        tile_count.reshape(1),
        tile_index.reshape(SLOTS),
        features,
        tile_values.reshape(SLOTS, TILE, TILE),
        weight,
        out_bias.reshape(1, F),
    )


def solution(mesh):
    in_specs = (
        P(("row", "col"), None),
        P("row", "col", None, None, None),
        P("row", "col", None),
        P("row", "col"),
        P(),
        P(),
    )
    return jax.shard_map(
        on_device, mesh=mesh, in_specs=in_specs, out_specs=P(("row", "col"), None), check_vma=False
    )
```
